128 devices in a mesh: clip: 4 (over x), rows: 32 (over y, z, core).
Axes of the slice: x: 4, y: 4, z: 4, core: 2. Of those that a mesh axis runs over, the one named last changes fastest.
Arguments:
- latents: bfloat16 [32, 320, 128, 128], P('clip', None, 'rows'), may hold values from -48 to 48
- time_embed: bfloat16 [32, 1280], P('clip'), may hold values from -6 to 6
- time_weight: bfloat16 [1280, 320], replicated, may hold values from -0.15625 to 0.15625
- gain_one: float32 [320], replicated, may hold values from 0.25 to 1.75
- shift_one: float32 [320], replicated, may hold values from -4 to 4
- conv_one: bfloat16 [3, 3, 320, 320], replicated, may hold values from -0.109375 to 0.109375
- bias_one: float32 [320], replicated, may hold values from -4 to 4
- gain_two: float32 [320], replicated, may hold values from 0.25 to 1.75
- shift_two: float32 [320], replicated, may hold values from -4 to 4
- conv_two: bfloat16 [3, 3, 320, 320], replicated, may hold values from -0.109375 to 0.109375
- bias_two: float32 [320], replicated, may hold values from -4 to 4
- send_order: int32 [4, 8192], P('clip', 'rows'), may hold values from 0 to 255, as said below
Outputs:
- block_out: bfloat16 [32, 320, 128, 128], P('clip', None, 'rows')
- student_tokens: bfloat16 [4, 320, 8192], P('clip', None, 'rows')
The draws below stay inside these ranges and needn't reach their ends.
Inputs may be any that keep to these rules, and one draw needn't show every extreme that they name: `send_order`: each block of 256 consecutive entries of a row (one band of a clip) is a permutation of 0 to 255.
All inputs are finite; a program needn't handle non-finite values.
Results may differ from the reference program's by a relative error of at most 0.0039.
Values may be sent and summed in bfloat16 or wider, within the bound.
A program may use at most 192 MiB of HBM per device.

```python
import math
import jax
import jax.numpy as jnp
from jax import lax

C = 320
GROUPS = 32
TEMB = 1280
WIDTH = 128
ROWS_DEV = 4
FRAMES = 8
CLIPS = 4
FRAMES_ALL = 32
HEIGHT = 128
PATCH_DEV = 256
PATCHES = 8192
N_ROWS = 32


def draw_latents(key, part):
    key = jax.random.fold_in(key, 11)
    key_base, key_rows, key_cols, key_chan = jax.random.split(key, 4)
    shape = (FRAMES_ALL, C, HEIGHT, WIDTH)
    position = jnp.arange(HEIGHT, dtype=jnp.float32) / max(HEIGHT - 1, 1)
    row_scale = (1.0 + 2.0 * position) * 0.5 * jnp.exp((jax.random.uniform(key_rows, (HEIGHT,)) - 0.5) * math.log(3.0))
    col_scale = jnp.exp((jax.random.uniform(key_cols, (WIDTH,)) - 0.5) * math.log(3.0))
    chan_scale = jnp.exp((jax.random.uniform(key_chan, (FRAMES_ALL, C)) - 0.5) * math.log(3.0))
    base = jnp.clip(jax.random.normal(key_base, shape), -6.0, 6.0)
    scale = chan_scale[:, :, None, None] * row_scale[None, None, :, None] * col_scale[None, None, None, :]
    return (base * scale).astype(jnp.bfloat16)


def draw_send_order(key, part):
    key = jax.random.fold_in(key, 23)
    keys = jax.random.split(key, CLIPS * N_ROWS)
    blocks = jax.vmap(lambda single: jax.random.permutation(single, PATCH_DEV))(keys)
    return blocks.reshape(CLIPS, PATCHES).astype(jnp.int32)


def level_of(stream_key, shape, pieces, smallest, top_value):
    def one(dim, blocks):
        draws = jax.random.uniform(jax.random.fold_in(jax.random.fold_in(stream_key, 6), dim), (blocks,), jnp.float32, smallest / len(pieces), top_value / len(pieces))
        return jnp.repeat(jnp.exp(draws), shape[dim] // blocks).reshape((-1,) + (1,) * (len(shape) - dim - 1))

    level = one(*pieces[0])
    for cut in pieces[1:]:
        level = level * one(*cut)
    return level


def gaussian(own_key, dims, scale, most, cuts=(), kind=jnp.bfloat16):
    array = jax.random.normal(own_key, dims, jnp.float32) * scale
    if len(cuts) > 0:
        array = level_of(own_key, dims, cuts, -0.22, 0.18) * array
    return jnp.clip(array, min=-most, max=most).astype(kind)


def setup_inputs(seed: int = 0) -> dict:
    arg_keys = jax.random.split(jax.random.key(seed), 13)
    latents = draw_latents(jax.random.fold_in(arg_keys[12], 71), 0)
    time_embed = gaussian(arg_keys[1], (FRAMES_ALL, TEMB), 1.0, 6.0, ((0, 4),))
    time_weight = gaussian(arg_keys[2], (TEMB, C), TEMB ** -0.5, 0.15625)
    gain_one = jnp.clip(1.0 + 0.15 * jax.random.normal(arg_keys[3], (C,), jnp.float32), 0.25, 1.75)
    shift_one = gaussian(arg_keys[4], (C,), 0.3, 4.0, (), jnp.float32)
    conv_one = gaussian(arg_keys[5], (3, 3, C, C), (9 * C) ** -0.5, 0.109375)
    bias_one = gaussian(arg_keys[6], (C,), 0.3, 4.0, (), jnp.float32)
    gain_two = jnp.clip(1.0 + 0.15 * jax.random.normal(arg_keys[7], (C,), jnp.float32), 0.25, 1.75)
    shift_two = gaussian(arg_keys[8], (C,), 0.3, 4.0, (), jnp.float32)
    conv_two = gaussian(arg_keys[9], (3, 3, C, C), (9 * C) ** -0.5, 0.109375)
    bias_two = gaussian(arg_keys[10], (C,), 0.3, 4.0, (), jnp.float32)
    send_order = draw_send_order(jax.random.fold_in(arg_keys[12], 71), 0)
    return dict(latents=latents, time_embed=time_embed, time_weight=time_weight, gain_one=gain_one, shift_one=shift_one, conv_one=conv_one, bias_one=bias_one, gain_two=gain_two, shift_two=shift_two, conv_two=conv_two, bias_two=bias_two, send_order=send_order)


def group_norm(values, gain, shift):
    channels, height, width = values.shape
    grouped = values.reshape(GROUPS, channels // GROUPS, height, width)
    group_mean = lax.optimization_barrier(jnp.mean(grouped, axis=(1, 2, 3), keepdims=True))
    group_var = lax.optimization_barrier(jnp.mean((grouped - group_mean) ** 2, axis=(1, 2, 3), keepdims=True))
    normed = ((grouped - group_mean) / jnp.sqrt(group_var + 1e-05)).reshape(channels, height, width)
    return normed * gain[:, None, None] + shift[:, None, None]

def convolve(active, weight):
    channels, height, width = active.shape
    padded = jnp.pad(active, ((0, 0), (1, 1), (1, 1)))
    total = jnp.zeros((channels, height * width), jnp.float32)
    for row_tap in range(3):
        for col_tap in range(3):
            window = padded[:, row_tap:row_tap + height, col_tap:col_tap + width].reshape(channels, height * width)
            total = total + jnp.dot(weight[row_tap, col_tap], window, preferred_element_type=jnp.float32)
    return total.reshape(channels, height, width)

def one_frame(inputs):
    frame, time_proj, gain_one, shift_one, conv_one, bias_one, gain_two, shift_two, conv_two, bias_two = inputs
    values = frame.astype(jnp.float32)
    act_one = jax.nn.silu(group_norm(values, gain_one, shift_one)).astype(jnp.bfloat16)
    hidden_one = (convolve(act_one, conv_one) + (bias_one + time_proj)[:, None, None]).astype(jnp.bfloat16)
    act_two = jax.nn.silu(group_norm(hidden_one.astype(jnp.float32), gain_two, shift_two)).astype(jnp.bfloat16)
    result = values + bias_two[:, None, None] + convolve(act_two, conv_two)
    channels, height, width = result.shape
    pooled = result.reshape(channels, height // 4, 4, width // 4, 4).mean(axis=(2, 4))
    return (result.astype(jnp.bfloat16), pooled.astype(jnp.bfloat16))

def reference(latents, time_embed, time_weight, gain_one, shift_one, conv_one, bias_one, gain_two, shift_two, conv_two, bias_two, send_order):
    time_act = jax.nn.silu(time_embed.astype(jnp.float32)).astype(jnp.bfloat16)
    time_proj = jnp.dot(time_act, time_weight, preferred_element_type=jnp.float32)

    def frame_fn(pair):
        frame, proj = pair
        return one_frame((frame, proj, gain_one, shift_one, conv_one, bias_one, gain_two, shift_two, conv_two, bias_two))
    block_out, pooled = lax.map(frame_fn, (latents, time_proj))
    pooled_rows = ROWS_DEV // 4
    pooled_cols = WIDTH // 4
    per_peer = PATCH_DEV // N_ROWS
    clip_tokens = []
    for clip_index in range(CLIPS):
        clip_pool = pooled[clip_index * FRAMES:(clip_index + 1) * FRAMES]
        banded = clip_pool.reshape(FRAMES, C, N_ROWS, pooled_rows, pooled_cols)
        banded = jnp.transpose(banded, (2, 1, 0, 3, 4)).reshape(N_ROWS, C, PATCH_DEV)
        order = send_order[clip_index].reshape(N_ROWS, PATCH_DEV).astype(jnp.int32)
        sent = jax.vmap(lambda cols, picks: jnp.take(cols, picks, axis=1))(banded, order)
        sent = sent.reshape(N_ROWS, C, N_ROWS, per_peer)
        clip_tokens.append(jnp.transpose(sent, (1, 2, 0, 3)).reshape(C, PATCHES))
    return (block_out, jnp.stack(clip_tokens, axis=0))
```

```python
import functools

import jax
import jax.numpy as jnp
from jax import lax
from jax.experimental import pallas as pl
from jax.experimental.pallas import tpu as pltpu
from jax.sharding import PartitionSpec as P

F32 = jnp.float32
BF16 = jnp.bfloat16
C = 320
CP = 384
GROUPS = 32
PER = C // GROUPS
W = 128
R = 4
FR = 8
ND = 32
NG = 2
FG = FR // NG
EXACT = lax.Precision.HIGHEST
MESH = pl.DeviceIdType.MESH


def dot(a, b, precision=None):
    return jnp.dot(a, b, preferred_element_type=F32, precision=precision)


def to_row(x):
    return jnp.sum(jnp.transpose(x), axis=0, keepdims=True)


def to_cols(row):
    return jnp.transpose(jnp.broadcast_to(row, (W, C)))


def group_lanes(first):
    chan = lax.broadcasted_iota(jnp.int32, (C, W), 0) // PER
    lane = lax.broadcasted_iota(jnp.int32, (C, W), 1)
    return jnp.where(chan + first == lane, 1.0, 0.0).astype(F32)


def group_rows():
    chan = lax.broadcasted_iota(jnp.int32, (W, C), 1) // PER
    lane = lax.broadcasted_iota(jnp.int32, (W, C), 0)
    return jnp.where(chan == lane, 1.0, 0.0).astype(F32)


def place_weights(raw, packed):
    for b in range(3):
        rows = slice(b * C, (b + 1) * C)
        for a in range(3):
            packed[rows, a * 256 : (a + 1) * 256] = raw[a * 3 + b, :, 0:256]
        packed[rows, 768:960] = jnp.concatenate([raw[a * 3 + b, :, 256:C] for a in range(3)], axis=1)


def conv_half(act, packed, half):
    lane = lax.broadcasted_iota(jnp.int32, (C, W), 1)
    at = [slice((half * 2 + a) * W, (half * 2 + a) * W + 2 * W) for a in range(3)]
    rhs = jnp.concatenate(
        [act[0:256, at[a]] for a in range(3)] + [act[256:C, at[a]] for a in range(3)], axis=0
    )
    y = [dot(packed[b * C : (b + 1) * C, :], rhs) for b in range(3)]
    rows = []
    for r in range(2):
        s = slice(r * W, (r + 1) * W)
        left = jnp.where(lane == 0, 0.0, pltpu.roll(y[0][:, s], 1, 1))
        right = jnp.where(lane == W - 1, 0.0, pltpu.roll(y[2][:, s], W - 1, 1))
        rows.append(y[1][:, s] + left + right)
    return rows


def main_kernel(
    lat, temb, tw, gain1, shift1, w1, bias1, gain2, shift2, w2, bias2, order,
    res, tok,
    lraw, wide, x6, h6, act, raw1, raw2, pk1, pk2, resbuf, psum,
    rowsum, pivot, sq, gath, msg, coef, offs, tsend, trecv,
    in_sem, w_sem, out_sem, halo_send, halo_recv, ag_send, ag_recv, tok_send, tok_recv,
):
    clip, me = lax.axis_index("clip"), lax.axis_index("rows")
    up, down = lax.rem(me + ND - 1, ND), lax.rem(me + 1, ND)
    n_local = float(PER * R * W)

    def partner(k):
        return lax.rem(me + k, ND)

    barrier = pltpu.get_barrier_semaphore()

    def greet(k, carry):
        pl.semaphore_signal(barrier, inc=1, device_id=(clip, partner(k)), device_id_type=MESH)
        return carry

    lax.fori_loop(1, ND, greet, 0)

    fetch = [pltpu.make_async_copy(lat.at[f], lraw.at[f], in_sem.at[f]) for f in range(FR)]
    for copy in fetch:
        copy.start()
    wfetch = [
        pltpu.make_async_copy(w1, raw1, w_sem.at[0]),
        pltpu.make_async_copy(w2, raw2, w_sem.at[1]),
    ]
    for copy in wfetch:
        copy.start()

    def halo_copies(stage, g):
        buf = (x6, h6)[stage]
        frames = pl.ds(g * FG, FG)
        return [
            pltpu.make_async_remote_copy(
                src_ref=buf.at[src, frames], dst_ref=buf.at[dst, frames],
                send_sem=halo_send.at[stage, g, i], recv_sem=halo_recv.at[stage, g, i],
                device_id=(clip, to), device_id_type=MESH,
            )
            for i, (src, dst, to) in enumerate(((1, 5, up), (4, 0, down)))
        ]

    def ag_copy(slot, k):
        return pltpu.make_async_remote_copy(
            src_ref=msg.at[slot], dst_ref=gath.at[slot, me],
            send_sem=ag_send.at[slot, k], recv_sem=ag_recv.at[slot, k],
            device_id=(clip, partner(k)), device_id_type=MESH,
        )

    def ag_start(slot):
        gath[slot, me] = msg[slot]

        def one(k, carry):
            ag_copy(slot, k).start()
            return carry

        lax.fori_loop(1, ND, one, 0)

    def ag_wait(slot):
        def one(k, carry):
            ag_copy(slot, k).wait()
            return carry

        lax.fori_loop(1, ND, one, 0)

    def stats(slot, stage, g):
        buf = (x6, h6)[stage]
        gl = group_lanes(0)
        mean = dot(rowsum[...], gl, EXACT) / n_local
        pivot[...] = dot(mean, group_rows(), EXACT)

        def one(j, carry):
            middle = to_cols(pivot[pl.ds(j, 1), :])
            total = None
            for r in range(R):
                d = buf[r + 1, g * FG + j].astype(F32) - middle
                total = d * d if total is None else total + d * d
            sq[pl.ds(j, 1), :] = to_row(total)
            return carry

        lax.fori_loop(0, FG, one, 0)
        msg[slot] = mean + dot(sq[...], group_lanes(GROUPS), EXACT)

    def coefs(slot, gain, shift):
        every = gath[slot]
        lane = lax.broadcasted_iota(jnp.int32, (8, W), 1)
        mean = jnp.sum(every, axis=0) * (1.0 / ND)
        away = every - mean[None]
        spread = jnp.sum(away * away, axis=0) * n_local
        inner = pltpu.roll(jnp.sum(every, axis=0), W - GROUPS, 1)
        var = (spread + inner) * (1.0 / (ND * n_local))
        valid = lane < GROUPS
        inv = jnp.where(valid, lax.rsqrt(jnp.where(valid, var, 1.0) + 1e-5), 0.0)
        gr = group_rows()
        scale = dot(inv, gr, EXACT) * gain[...]
        offset = shift[...] - dot(jnp.where(valid, mean, 0.0), gr, EXACT) * scale
        coef[0] = scale * 0.5
        coef[1] = offset * 0.5

    def activate(buf, f, j):
        sc = to_cols(coef[0, pl.ds(j, 1), :])
        sh = to_cols(coef[1, pl.ds(j, 1), :])
        for row in range(R + 2):
            h = buf[row, f].astype(F32) * sc + sh
            a = h * jnp.tanh(h) + h
            if row == 0:
                a = jnp.where(me > 0, a, 0.0)
            if row == R + 1:
                a = jnp.where(me < ND - 1, a, 0.0)
            act[:, row * W : (row + 1) * W] = a.astype(BF16)

    rowsum[...] = jnp.zeros((8, C), F32)
    sq[...] = jnp.zeros((8, C), F32)

    def split(f, carry):
        pltpu.make_async_copy(lat.at[f], lraw.at[f], in_sem.at[f]).wait()
        wide[...] = lraw[f].astype(F32)
        total = None
        for r in range(R):
            x = wide[pl.ds(r, C, stride=R), :]
            x6[r + 1, f] = x.astype(BF16)
            total = x if total is None else total + x
        rowsum[pl.ds(lax.rem(f, FG), 1), :] = to_row(total)
        return carry

    for g in range(NG):
        lax.fori_loop(g * FG, (g + 1) * FG, split, 0)
        if g == 0:
            pl.semaphore_wait(barrier, ND - 1)
        for copy in halo_copies(0, g):
            copy.start()
        stats(g, 0, g)
        ag_start(g)

    embed = temb[...].astype(F32)
    tact = (embed / (1.0 + jnp.exp(-embed))).astype(BF16)
    offs[...] = dot(tact, tw[...]) + bias1[...]
    wfetch[0].wait()
    place_weights(raw1, pk1)
    wfetch[1].wait()
    place_weights(raw2, pk2)

    for g in range(NG):
        ag_wait(g)
        for copy in halo_copies(0, g):
            copy.wait()
        coefs(g, gain1, shift1)

        def first(j, carry):
            f = g * FG + j
            activate(x6, f, j)
            off = to_cols(offs[pl.ds(f, 1), :])
            total = None
            for half in range(2):
                for i, y in enumerate(conv_half(act, pk1, half)):
                    h = (y + off).astype(BF16)
                    h6[half * 2 + i + 1, f] = h
                    h = h.astype(F32)
                    total = h if total is None else total + h
            rowsum[pl.ds(j, 1), :] = to_row(total)
            return carry

        lax.fori_loop(0, FG, first, 0)
        for copy in halo_copies(1, g):
            copy.start()
        stats(NG + g, 1, g)
        ag_start(NG + g)

    tail = to_cols(bias2[...])

    for g in range(NG):
        ag_wait(NG + g)
        for copy in halo_copies(1, g):
            copy.wait()
        coefs(NG + g, gain2, shift2)

        def second(j, carry):
            f = g * FG + j
            activate(h6, f, j)
            total = None
            for half in range(2):
                for i, y in enumerate(conv_half(act, pk2, half)):
                    r = half * 2 + i
                    v = y + (x6[r + 1, f].astype(F32) + tail)
                    resbuf[f, r] = v.astype(BF16)
                    total = v if total is None else total + v
            psum[f] = total
            pltpu.make_async_copy(resbuf.at[f], res.at[f], out_sem.at[f]).start()
            return carry

        lax.fori_loop(0, FG, second, 0)

    lanes = FR * W
    spot = lax.broadcasted_iota(jnp.int32, (lanes, 256), 0) // 4
    col = lax.broadcasted_iota(jnp.int32, (lanes, 256), 1)
    pool = jnp.where(spot == col, 1.0 / 16.0, 0.0).astype(BF16)
    sums = jnp.concatenate([psum[f] for f in range(FR)], axis=1)
    high = sums.astype(BF16)
    rest = sums - high.astype(F32)
    mid = rest.astype(BF16)
    low = (rest - mid.astype(F32)).astype(BF16)
    pooled = (dot(high, pool) + dot(mid, pool) + dot(low, pool)).astype(BF16)
    patch = lax.broadcasted_iota(jnp.int32, (256, 256), 0)
    pick = jnp.where(patch == order[...], 1.0, 0.0).astype(BF16)
    chosen = dot(pooled, pick)
    placed = jnp.transpose(jnp.concatenate([chosen, jnp.zeros((CP - C, 256), F32)], axis=0))
    placed = placed.reshape(ND, 8, CP)
    lower = jnp.concatenate([placed[:, :, 256:CP], jnp.zeros((ND, 8, 128), F32)], axis=2)
    tsend[...] = jnp.concatenate([placed[:, :, 0:256], lower], axis=1).astype(BF16)
    trecv[me] = tsend[me]

    def tok_copy(k):
        return pltpu.make_async_remote_copy(
            src_ref=tsend.at[partner(k)], dst_ref=trecv.at[me],
            send_sem=tok_send.at[k], recv_sem=tok_recv.at[k],
            device_id=(clip, partner(k)), device_id_type=MESH,
        )

    def tok_start(k, carry):
        tok_copy(k).start()
        return carry

    def tok_wait(k, carry):
        tok_copy(k).wait()
        return carry

    lax.fori_loop(1, ND, tok_start, 0)
    lax.fori_loop(1, ND, tok_wait, 0)
    tok[...] = trecv[...]

    def drain(f, carry):
        pltpu.make_async_copy(resbuf.at[f], res.at[f], out_sem.at[f]).wait()
        return carry

    lax.fori_loop(0, FR, drain, 0)


def finish_kernel(res, tok, out, student, wide):
    for r in range(R):
        wide[pl.ds(r, C, stride=R), :] = res[0, r].astype(F32)
    out[0] = wide[...].astype(BF16)

    @pl.when(pl.program_id(0) == 0)
    def _():
        t = tok[...].astype(F32)
        top = jnp.transpose(t[:, 0:8, :].reshape(256, 256))
        low = jnp.transpose(t[:, 8:16, 0:128].reshape(256, 128))
        student[0] = jnp.concatenate([top, low[0 : C - 256]], axis=0).astype(BF16)


def body(lat, temb, tw, gain1, shift1, w1, bias1, gain2, shift2, w2, bias2, order):
    vm = pl.BlockSpec(memory_space=pltpu.VMEM)
    anyspace = pl.BlockSpec(memory_space=pl.ANY)
    dma = pltpu.SemaphoreType.DMA
    row = lambda v: v.reshape(1, C)
    res, tok = pl.pallas_call(
        main_kernel,
        out_shape=(
            jax.ShapeDtypeStruct((FR, R, C, W), BF16),
            jax.ShapeDtypeStruct((ND, 16, 256), BF16),
        ),
        in_specs=[anyspace, vm, vm, vm, vm, anyspace, vm, vm, vm, anyspace, vm, vm],
        out_specs=(anyspace, vm),
        scratch_shapes=[
            pltpu.VMEM((FR, C * R, W), BF16),
            pltpu.VMEM((C * R, W), F32),
            pltpu.VMEM((R + 2, FR, C, W), BF16),
            pltpu.VMEM((R + 2, FR, C, W), BF16),
            pltpu.VMEM((C, (R + 2) * W), BF16),
            pltpu.VMEM((9, C, C), BF16),
            pltpu.VMEM((9, C, C), BF16),
            pltpu.VMEM((3 * C, 3 * C), BF16),
            pltpu.VMEM((3 * C, 3 * C), BF16),
            pltpu.VMEM((FR, R, C, W), BF16),
            pltpu.VMEM((FR, C, W), F32),
            pltpu.VMEM((8, C), F32),
            pltpu.VMEM((8, C), F32),
            pltpu.VMEM((8, C), F32),
            pltpu.VMEM((2 * NG, ND, 8, W), F32),
            pltpu.VMEM((2 * NG, 8, W), F32),
            pltpu.VMEM((2, 8, C), F32),
            pltpu.VMEM((FR, C), F32),
            pltpu.VMEM((ND, 16, 256), BF16),
            pltpu.VMEM((ND, 16, 256), BF16),
            dma((FR,)),
            dma((2,)),
            dma((FR,)),
            dma((2, NG, 2)),
            dma((2, NG, 2)),
            dma((2 * NG, ND)),
            dma((2 * NG, ND)),
            dma((ND,)),
            dma((ND,)),
        ],
        compiler_params=pltpu.CompilerParams(
            collective_id=0, has_side_effects=True, vmem_limit_bytes=56 * 2**20
        ),
        name="block",
    )(
        lat.reshape(FR, C * R, W), temb, tw, row(gain1), row(shift1), w1.reshape(9, C, C), row(bias1),
        row(gain2), row(shift2), w2.reshape(9, C, C), row(bias2), order,
    )
    out, student = pl.pallas_call(
        finish_kernel,
        grid=(FR,),
        out_shape=(
            jax.ShapeDtypeStruct((FR, C * R, W), BF16),
            jax.ShapeDtypeStruct((1, C, 256), BF16),
        ),
        in_specs=[
            pl.BlockSpec((1, R, C, W), lambda f: (f, 0, 0, 0)),
            pl.BlockSpec((ND, 16, 256), lambda f: (0, 0, 0)),
        ],
        out_specs=(
            pl.BlockSpec((1, C * R, W), lambda f: (f, 0, 0)),
            pl.BlockSpec((1, C, 256), lambda f: (0, 0, 0)),
        ),
        scratch_shapes=[pltpu.VMEM((C * R, W), F32)],
        name="finish",
    )(res, tok)
    return out.reshape(FR, C, R, W), student


def solution(mesh):
    return jax.shard_map(
        body,
        mesh=mesh,
        in_specs=(
            P("clip", None, "rows", None),
            P("clip", None),
            P(), P(), P(), P(), P(), P(), P(), P(), P(),
            P("clip", "rows"),
        ),
        out_specs=(P("clip", None, "rows", None), P("clip", None, "rows")),
        check_vma=False,
    )
```

```python
import functools

import jax
import jax.numpy as jnp
from jax import lax
from jax.experimental import pallas as pl
from jax.experimental.pallas import tpu as pltpu
from jax.sharding import PartitionSpec as P

F32 = jnp.float32
BF16 = jnp.bfloat16
C = 320
GROUPS = 32
PER = C // GROUPS
W = 128
TEMB = 1280
R = 4
FR = 8
ND = 32
FG = 4
DEPTH = 3 * C + 32
MESH = pl.DeviceIdType.MESH


def dot(a, b):
    return jnp.dot(a, b, preferred_element_type=F32)


def dot_nt(a, b):
    return lax.dot_general(a, b, (((1,), (1,)), ((), ())), preferred_element_type=F32)


def to_row(x):
    return jnp.sum(jnp.transpose(x), axis=0, keepdims=True)


def to_cols(row):
    return jnp.transpose(jnp.broadcast_to(row, (W, C)))


def split3(a):
    high = a.astype(BF16)
    rest = a - high.astype(F32)
    mid = rest.astype(BF16)
    return jnp.concatenate([high, mid, (rest - mid.astype(F32)).astype(BF16)], axis=0)


def exact(a, ones):
    m = a.shape[0]
    y = dot(split3(a), ones)
    return y[0:m] + y[m : 2 * m] + y[2 * m : 3 * m]


def group_of(shape, dim):
    i = lax.broadcasted_iota(jnp.int32, shape, dim)
    return lax.div(i, PER)


def where_one(flags):
    return jnp.where(flags, 1.0, 0.0).astype(BF16)


def place_weights(raw, packed, offsets):
    parts = split3(offsets).astype(F32)
    parts = jnp.transpose(jnp.concatenate([parts, jnp.zeros((W - 24, C), F32)], axis=0))
    parts = parts[:, 0:32].astype(BF16)
    for b in range(3):
        rows = slice(b * C, (b + 1) * C)
        for a in range(3):
            packed[rows, a * 256 : (a + 1) * 256] = raw[a * 3 + b, :, 0:256]
        rest = [raw[a * 3 + b, :, 256:C] for a in range(3)]
        rest.append(parts if b == 1 else jnp.zeros((C, 32), BF16))
        packed[rows, 768:DEPTH] = jnp.concatenate(rest, axis=1)


def conv_half(act, packed, f, half):
    lane = lax.broadcasted_iota(jnp.int32, (C, W), 1)
    row = lax.broadcasted_iota(jnp.int32, (32, 2 * W), 0)
    mine = where_one((lax.rem(row, 8) == f) & (row < 24))
    at = [slice((half * 2 + a) * W, (half * 2 + a) * W + 2 * W) for a in range(3)]
    rhs = jnp.concatenate(
        [act[0:256, at[a]] for a in range(3)] + [act[256:C, at[a]] for a in range(3)] + [mine], axis=0
    )
    y = [dot(packed[b * C : (b + 1) * C, :], rhs) for b in range(3)]
    rows = []
    for r in range(2):
        s = slice(r * W, (r + 1) * W)
        left = jnp.where(lane == 0, 0.0, pltpu.roll(y[0][:, s], 1, 1))
        right = jnp.where(lane == W - 1, 0.0, pltpu.roll(y[2][:, s], W - 1, 1))
        rows.append(y[1][:, s] + left + right)
    return rows


def main_kernel(
    lat_in, temb_in, tw_in, gain1_in, shift1_in, w1_in, bias1_in, gain2_in, shift2_in, w2_in, bias2_in, order_in,
    res, tok,
    lraw, temb, tw, gain1, shift1, raw1, bias1, gain2, shift2, raw2, bias2, order,
    wide, wide2, x6, h6, act0, act1, pk1, pk2, resbuf, obuf, sums,
    means, sqs, gath, msg, coef, same, lanes_a, lanes_b, rows_g, orders, chosen, tsend, trecv,
    in_sem, small_sem, out_sem, halo_send, halo_recv, ag_send, ag_recv, tok_send, tok_recv,
):
    clip, me = lax.axis_index("clip"), lax.axis_index("rows")
    up, down = lax.rem(me + ND - 1, ND), lax.rem(me + 1, ND)
    n_local = float(PER * R * W)

    def partner(k):
        return lax.rem(me + k, ND)

    fetch = [pltpu.make_async_copy(lat_in.at[f], lraw.at[f], in_sem.at[f]) for f in range(FR)]
    for copy in fetch:
        copy.start()

    barrier = pltpu.get_barrier_semaphore()

    def greet(k, carry):
        pl.semaphore_signal(barrier, inc=1, device_id=(clip, partner(k)), device_id_type=MESH)
        return carry

    lax.fori_loop(1, ND, greet, 0)

    others = [
        (temb_in, temb), (tw_in, tw), (bias1_in, bias1), (w1_in, raw1), (gain1_in, gain1), (shift1_in, shift1),
        (bias2_in, bias2), (w2_in, raw2), (gain2_in, gain2), (shift2_in, shift2), (order_in, order),
    ]
    others = [pltpu.make_async_copy(a, b, small_sem.at[i]) for i, (a, b) in enumerate(others)]

    def halo_copies(stage, pair):
        buf = (x6, h6)[stage]
        frames = pl.ds(pair * 2, 2)
        return [
            pltpu.make_async_remote_copy(
                src_ref=buf.at[src, frames], dst_ref=buf.at[dst, frames],
                send_sem=halo_send.at[stage, pair, i], recv_sem=halo_recv.at[stage, pair, i],
                device_id=(clip, to), device_id_type=MESH,
            )
            for i, (src, dst, to) in enumerate(((1, 5, up), (4, 0, down)))
        ]

    def halo_start(stage, pair):
        for copy in halo_copies(stage, pair):
            copy.start()

    def halo_wait(stage, pair):
        for copy in halo_copies(stage, pair):
            copy.wait()

    def ag_copy(slot, k):
        return pltpu.make_async_remote_copy(
            src_ref=msg.at[slot], dst_ref=gath.at[slot, me],
            send_sem=ag_send.at[slot, k], recv_sem=ag_recv.at[slot, k],
            device_id=(clip, partner(k)), device_id_type=MESH,
        )

    def gather_start(slot):
        for k in range(1, ND):
            ag_copy(slot, k).start()
        gath[slot, me] = msg[slot]

    def gather_end(slot):
        def one(k, carry):
            ag_copy(slot, k).wait()
            return carry

        lax.fori_loop(1, ND, one, 0)
        every = gath[slot]
        lane = lax.broadcasted_iota(jnp.int32, (8, W), 1)
        total = jnp.sum(every, axis=0)
        mean = total * (1.0 / ND)
        away = every - mean[None]
        spread = jnp.sum(away * away, axis=0) * n_local
        square = total + pltpu.roll(spread, GROUPS, 1)
        return jnp.where(lane < GROUPS, mean, jnp.where(lane < 2 * GROUPS, square, 0.0))

    def channel_stats(j, xs):
        total = (xs[0] + xs[1]) + (xs[2] + xs[3])
        middle = total * (1.0 / R)
        away = None
        for x in xs:
            d = x - middle
            away = d * d if away is None else away + d * d
        mean = to_row(total) * (1.0 / (R * W))
        d = middle - to_cols(mean)
        means[pl.ds(j, 1), :] = mean
        sqs[pl.ds(j, 1), :] = to_row(away + d * d * float(R))

    def channel_sums(j, xs):
        total = (xs[0] + xs[1]) + (xs[2] + xs[3])
        square = (xs[0] * xs[0] + xs[1] * xs[1]) + (xs[2] * xs[2] + xs[3] * xs[3])
        mean = to_row(total) * (1.0 / (R * W))
        means[pl.ds(j, 1), :] = mean
        sqs[pl.ds(j, 1), :] = to_row(square) - mean * mean * float(R * W)

    def stats(slot):
        mean = means[...]
        d = mean - exact(mean, same[...]) * (1.0 / PER)
        inner = sqs[...] + d * d * float(R * W)
        msg[slot] = exact(mean, lanes_a[...]) * (1.0 / PER) + exact(inner, lanes_b[...])

    def coefs(slot, gain, shift):
        both = gather_end(slot)
        valid = lax.broadcasted_iota(jnp.int32, (8, W), 1) < GROUPS
        var = jnp.maximum(pltpu.roll(both, W - GROUPS, 1), 0.0) * (1.0 / (ND * n_local))
        inv = jnp.where(valid, lax.rsqrt(var + 1e-5), 0.0)
        both = exact(jnp.concatenate([inv, jnp.where(valid, both, 0.0)], axis=0), rows_g[...])
        scale = both[0:8] * gain[...].reshape(1, C)
        coef[0] = scale * 0.5
        coef[1] = (shift[...].reshape(1, C) - both[8:16] * scale) * 0.5

    def activate(buf, act, f, j):
        sc = to_cols(coef[0, pl.ds(j, 1), :])
        sh = to_cols(coef[1, pl.ds(j, 1), :])
        for row in range(R + 2):
            h = buf[row, f].astype(F32) * sc + sh
            a = h * jnp.tanh(h) + h
            if row == 0:
                a = jnp.where(me > 0, a, 0.0)
            if row == R + 1:
                a = jnp.where(me < ND - 1, a, 0.0)
            act[:, row * W : (row + 1) * W] = a.astype(BF16)

    acts = (act0, act1)

    def split(i, carry):
        for p, buf in enumerate((wide, wide2)):
            f = i * 2 + p
            pltpu.make_async_copy(lat_in.at[f], lraw.at[f], in_sem.at[f]).wait()
        for p, buf in enumerate((wide, wide2)):
            f = i * 2 + p
            buf[...] = lraw[f].astype(F32)
            xs = [buf[pl.ds(r, C, stride=R), :] for r in range(R)]
            for r in range(R):
                x6[r + 1, f] = xs[r].astype(BF16)
            channel_stats(f, xs)
        return carry

    lax.fori_loop(0, 1, split, 0)
    pl.semaphore_wait(barrier, ND - 1)
    halo_start(0, 0)
    lax.fori_loop(1, FR // 2, split, 0)
    for copy in others:
        copy.start()
    same[...] = where_one(group_of((C, C), 0) == group_of((C, C), 1))
    lane = lax.broadcasted_iota(jnp.int32, (C, W), 1)
    lanes_a[...] = where_one(group_of((C, W), 0) == lane)
    lanes_b[...] = where_one(group_of((C, W), 0) + GROUPS == lane)
    stats(0)
    gather_start(0)
    for pair in range(1, FR // 2):
        halo_start(0, pair)

    rows_g[...] = where_one(group_of((W, C), 1) == lax.broadcasted_iota(jnp.int32, (W, C), 0))
    for copy in others:
        copy.wait()
    embed = temb[...].astype(F32)
    tact = (embed / (1.0 + jnp.exp(-embed))).astype(BF16)
    place_weights(raw1, pk1, dot_nt(tact, tw[...]) + bias1[...].reshape(1, C))
    place_weights(raw2, pk2, jnp.broadcast_to(bias2[...].reshape(1, C), (8, C)))
    orders[...] = jnp.transpose(jnp.broadcast_to(order[...].astype(F32), (2 * W, 256))).astype(jnp.int32)
    chosen[...] = jnp.zeros((256, C), F32)

    coefs(0, gain1, shift1)
    halo_wait(0, 0)
    activate(x6, act0, 0, 0)
    for f in range(FR):
        if f + 1 < FR:
            if f % 2 == 1:
                halo_wait(0, (f + 1) // 2)
            activate(x6, acts[(f + 1) % 2], f + 1, f + 1)
        xs = []
        for half in range(2):
            for y in conv_half(acts[f % 2], pk1, f, half):
                h = y.astype(BF16)
                h6[len(xs) + 1, f] = h
                xs.append(h.astype(F32))
        channel_sums(f % FG, xs)
        if f == FG - 1:
            stats(1)
            gather_start(1)
        if f % 2 == 1 and f < FR - 1:
            halo_start(1, f // 2)
    stats(2)

    quarter = lax.div(lax.broadcasted_iota(jnp.int32, (256, 2 * W), 1), 4)
    coefs(1, gain2, shift2)
    halo_wait(1, 0)
    gather_start(2)
    halo_start(1, FR // 2 - 1)
    activate(h6, act0, 0, 0)
    for f in range(FR):
        if f + 1 < FR:
            if f + 1 == FG:
                coefs(2, gain2, shift2)
            if f % 2 == 1:
                halo_wait(1, (f + 1) // 2)
            activate(h6, acts[(f + 1) % 2], f + 1, (f + 1) % FG)
        total = None
        for half in range(2):
            for i, y in enumerate(conv_half(acts[f % 2], pk2, f, half)):
                r = half * 2 + i
                v = y + x6[r + 1, f].astype(F32)
                resbuf[f, r] = v.astype(BF16)
                total = v if total is None else total + v
        high = total.astype(BF16)
        cols = slice(f % 2 * W, f % 2 * W + W)
        sums[0, :, cols] = high
        sums[1, :, cols] = (total - high.astype(F32)).astype(BF16)
        if f % 2 == 1:
            pick = jnp.where(orders[...] == quarter + f // 2 * (W // 2), 1.0 / 16.0, 0.0).astype(BF16)
            chosen[...] += dot_nt(pick, sums[0]) + dot_nt(pick, sums[1])

    placed = chosen[...].reshape(ND, 8, C)
    lower = jnp.concatenate([placed[:, :, 256:C], jnp.zeros((ND, 8, 512 - C), F32)], axis=2)
    tsend[...] = jnp.concatenate([placed[:, :, 0:256], lower], axis=1).astype(BF16)

    def tok_copy(k):
        return pltpu.make_async_remote_copy(
            src_ref=tsend.at[partner(k)], dst_ref=trecv.at[me],
            send_sem=tok_send.at[k], recv_sem=tok_recv.at[k],
            device_id=(clip, partner(k)), device_id_type=MESH,
        )

    def tok_wait(k, carry):
        tok_copy(k).wait()
        return carry

    for k in range(1, ND):
        tok_copy(k).start()
    trecv[me] = tsend[me]

    def put(f):
        return pltpu.make_async_copy(obuf.at[f], res.at[f], out_sem.at[f])

    for f in range(FR):
        buf = (wide, wide2)[f % 2]
        for r in range(R):
            buf[pl.ds(r, C, stride=R), :] = resbuf[f, r].astype(F32)
        obuf[f] = buf[...].astype(BF16)
        put(f).start()

    lax.fori_loop(1, ND, tok_wait, 0)
    last = pltpu.make_async_copy(trecv, tok, small_sem.at[0])
    last.start()
    for f in range(FR):
        put(f).wait()
    last.wait()


def finish_kernel(res, tok, out, student, rbuf, tbuf, sbuf, in_sem, out_sem):
    fetch = [pltpu.make_async_copy(res.at[f], rbuf.at[f], in_sem.at[f]) for f in range(FR)]
    put = [pltpu.make_async_copy(rbuf.at[f], out.at[f], out_sem.at[f]) for f in range(FR)]
    tokens = pltpu.make_async_copy(tok, tbuf, in_sem.at[FR])
    for copy in fetch:
        copy.start()
    tokens.start()
    for f in range(FR // 2):
        fetch[f].wait()
        put[f].start()
    tokens.wait()
    t = tbuf[...].astype(F32)
    top = jnp.transpose(t[:, 0:8, :].reshape(256, 256))
    low = jnp.transpose(t[:, 8:16, 0:128].reshape(256, 128))
    sbuf[...] = jnp.concatenate([top, low[0 : C - 256]], axis=0).astype(BF16)
    put.append(pltpu.make_async_copy(sbuf, student.at[0], out_sem.at[FR]))
    put[FR].start()
    for f in range(FR // 2, FR):
        fetch[f].wait()
        put[f].start()
    for copy in put:
        copy.wait()


def body(lat, temb, tw, gain1, shift1, w1, bias1, gain2, shift2, w2, bias2, order):
    anyspace = pl.BlockSpec(memory_space=pl.ANY)
    dma = pltpu.SemaphoreType.DMA
    vec = pltpu.VMEM((C,), F32)
    raw = pltpu.VMEM((9, C, C), BF16)
    pairs = dma((2, FR // 2, 2))
    res, tok = pl.pallas_call(
        main_kernel,
        out_shape=(
            jax.ShapeDtypeStruct((FR, C * R, W), BF16),
            jax.ShapeDtypeStruct((ND, 16, 256), BF16),
        ),
        in_specs=[anyspace] * 12,
        out_specs=(anyspace, anyspace),
        scratch_shapes=[
            pltpu.VMEM((FR, C * R, W), BF16),
            pltpu.VMEM((FR, TEMB), BF16),
            pltpu.VMEM((C, TEMB), BF16),
            vec, vec, raw, vec, vec, vec, raw, vec,
            pltpu.VMEM((1, 256), jnp.int32),
            pltpu.VMEM((C * R, W), F32),
            pltpu.VMEM((C * R, W), F32),
            pltpu.VMEM((R + 2, FR, C, W), BF16),
            pltpu.VMEM((R + 2, FR, C, W), BF16),
            pltpu.VMEM((C, (R + 2) * W), BF16),
            pltpu.VMEM((C, (R + 2) * W), BF16),
            pltpu.VMEM((3 * C, DEPTH), BF16),
            pltpu.VMEM((3 * C, DEPTH), BF16),
            pltpu.VMEM((FR, R, C, W), BF16),
            pltpu.VMEM((FR, C * R, W), BF16),
            pltpu.VMEM((2, C, 2 * W), BF16),
            pltpu.VMEM((8, C), F32),
            pltpu.VMEM((8, C), F32),
            pltpu.VMEM((3, ND, 8, W), F32),
            pltpu.VMEM((3, 8, W), F32),
            pltpu.VMEM((2, 8, C), F32),
            pltpu.VMEM((C, C), BF16),
            pltpu.VMEM((C, W), BF16),
            pltpu.VMEM((C, W), BF16),
            pltpu.VMEM((W, C), BF16),
            pltpu.VMEM((256, 2 * W), jnp.int32),
            pltpu.VMEM((256, C), F32),
            pltpu.VMEM((ND, 16, 256), BF16),
            pltpu.VMEM((ND, 16, 256), BF16),
            dma((FR,)), dma((11,)), dma((FR,)), pairs, pairs,
            dma((3, ND)), dma((3, ND)), dma((ND,)), dma((ND,)),
        ],
        compiler_params=pltpu.CompilerParams(
            collective_id=0, has_side_effects=True, vmem_limit_bytes=56 * 2**20
        ),
        name="block",
    )(
        lat.reshape(FR, C * R, W), temb, tw.T, gain1, shift1, w1.reshape(9, C, C), bias1,
        gain2, shift2, w2.reshape(9, C, C), bias2, order,
    )
    out, student = pl.pallas_call(
        finish_kernel,
        out_shape=(
            jax.ShapeDtypeStruct((FR, C * R, W), BF16),
            jax.ShapeDtypeStruct((1, C, 256), BF16),
        ),
        in_specs=[anyspace, anyspace],
        out_specs=(anyspace, anyspace),
        scratch_shapes=[
            pltpu.VMEM((FR, C * R, W), BF16),
            pltpu.VMEM((ND, 16, 256), BF16),
            pltpu.VMEM((C, 256), BF16),
            dma((FR + 1,)),
            dma((FR + 1,)),
        ],
        compiler_params=pltpu.CompilerParams(vmem_limit_bytes=56 * 2**20),
        name="finish",
    )(res, tok)
    return out.reshape(FR, C, R, W), student


def solution(mesh):
    return jax.shard_map(
        body,
        mesh=mesh,
        in_specs=(
            P("clip", None, "rows", None),
            P("clip", None),
            P(), P(), P(), P(), P(), P(), P(), P(), P(),
            P("clip", "rows"),
        ),
        out_specs=(P("clip", None, "rows", None), P("clip", None, "rows")),
        check_vma=False,
    )
```

```python
import functools

import jax
import jax.numpy as jnp
from jax import lax
from jax.experimental import pallas as pl
from jax.experimental.pallas import tpu as pltpu
from jax.sharding import PartitionSpec as P

F32 = jnp.float32
BF16 = jnp.bfloat16
C = 320
GROUPS = 32
PER = C // GROUPS
W = 128
TEMB = 1280
R = 4
FR = 8
ND = 32
EDGES = (((0, 2), (2, 1), (3, 2), (5, 2), (7, 1)), ((0, 2), (2, 2), (4, 2), (6, 2)))
SLOT_TWO = (1, 1, 1, 1, 2, 2, 3, 3)
SLOTS = 4
DEPTH = 3 * C + 32
MESH = pl.DeviceIdType.MESH


def dot(a, b):
    return jnp.dot(a, b, preferred_element_type=F32)


def dot_nt(a, b):
    return lax.dot_general(a, b, (((1,), (1,)), ((), ())), preferred_element_type=F32)


def to_row(x):
    return jnp.sum(jnp.transpose(x), axis=0, keepdims=True)


def to_cols(row):
    return jnp.transpose(jnp.broadcast_to(row, (W, C)))


def split3(a):
    high = a.astype(BF16)
    rest = a - high.astype(F32)
    mid = rest.astype(BF16)
    return jnp.concatenate([high, mid, (rest - mid.astype(F32)).astype(BF16)], axis=0)


def exact(a, ones):
    m = a.shape[0]
    y = dot(split3(a), ones)
    return y[0:m] + y[m : 2 * m] + y[2 * m : 3 * m]


def group_of(shape, dim):
    i = lax.broadcasted_iota(jnp.int32, shape, dim)
    return lax.div(i, PER)


def where_one(flags):
    return jnp.where(flags, 1.0, 0.0).astype(BF16)


def place_weights(raw, packed, offsets):
    parts = split3(offsets).astype(F32)
    parts = jnp.transpose(jnp.concatenate([parts, jnp.zeros((W - 24, C), F32)], axis=0))
    parts = parts[:, 0:32].astype(BF16)
    for b in range(3):
        rows = slice(b * C, (b + 1) * C)
        for a in range(3):
            packed[rows, a * 256 : (a + 1) * 256] = raw[a * 3 + b, :, 0:256]
        rest = [raw[a * 3 + b, :, 256:C] for a in range(3)]
        rest.append(parts if b == 1 else jnp.zeros((C, 32), BF16))
        packed[rows, 768:DEPTH] = jnp.concatenate(rest, axis=1)


def conv_half(act, packed, f, half):
    lane = lax.broadcasted_iota(jnp.int32, (C, W), 1)
    row = lax.broadcasted_iota(jnp.int32, (32, 2 * W), 0)
    mine = where_one((lax.rem(row, 8) == f) & (row < 24))
    at = [slice((half * 2 + a) * W, (half * 2 + a) * W + 2 * W) for a in range(3)]
    rhs = jnp.concatenate(
        [act[0:256, at[a]] for a in range(3)] + [act[256:C, at[a]] for a in range(3)] + [mine], axis=0
    )
    y = [dot(packed[b * C : (b + 1) * C, :], rhs) for b in range(3)]
    rows = []
    for r in range(2):
        s = slice(r * W, (r + 1) * W)
        left = jnp.where(lane == 0, 0.0, pltpu.roll(y[0][:, s], 1, 1))
        right = jnp.where(lane == W - 1, 0.0, pltpu.roll(y[2][:, s], W - 1, 1))
        rows.append(y[1][:, s] + left + right)
    return rows


def main_kernel(
    lat_in, temb_in, tw_in, gain1_in, shift1_in, w1_in, bias1_in, gain2_in, shift2_in, w2_in, bias2_in, order_in,
    res, tok,
    lraw, temb, tw, gain1, shift1, raw1, bias1, gain2, shift2, raw2, bias2, order,
    wide, wide2, x6, h6, act0, act1, pk1, pk2, resbuf, sums,
    means, sqs, gath, msg, coef, same, lanes_a, lanes_b, rows_g, orders, chosen, tsend, trecv,
    in_sem, small_sem, halo_send, halo_recv, ag_send, ag_recv, tok_send, tok_recv,
):
    clip, me = lax.axis_index("clip"), lax.axis_index("rows")
    up, down = lax.rem(me + ND - 1, ND), lax.rem(me + 1, ND)
    n_local = float(PER * R * W)

    def partner(k):
        return lax.rem(me + k, ND)

    fetch = [pltpu.make_async_copy(lat_in.at[f], lraw.at[f], in_sem.at[f]) for f in range(FR)]
    for copy in fetch:
        copy.start()

    barrier = pltpu.get_barrier_semaphore()

    def greet(k, carry):
        pl.semaphore_signal(barrier, inc=1, device_id=(clip, partner(k)), device_id_type=MESH)
        return carry

    lax.fori_loop(1, ND, greet, 0)

    others = [
        (temb_in, temb), (tw_in, tw), (bias1_in, bias1), (w1_in, raw1), (gain1_in, gain1), (shift1_in, shift1),
        (bias2_in, bias2), (w2_in, raw2), (gain2_in, gain2), (shift2_in, shift2), (order_in, order),
    ]
    others = [pltpu.make_async_copy(a, b, small_sem.at[i]) for i, (a, b) in enumerate(others)]

    def halo_copies(stage, n):
        buf = (x6, h6)[stage]
        frames = pl.ds(*EDGES[stage][n])
        return [
            pltpu.make_async_remote_copy(
                src_ref=buf.at[src, frames], dst_ref=buf.at[dst, frames],
                send_sem=halo_send.at[stage, n, i], recv_sem=halo_recv.at[stage, n, i],
                device_id=(clip, to), device_id_type=MESH,
            )
            for i, (src, dst, to) in enumerate(((1, 5, up), (4, 0, down)))
        ]

    def halo_start(stage, n):
        for copy in halo_copies(stage, n):
            copy.start()

    def halo_wait(stage, n):
        for copy in halo_copies(stage, n):
            copy.wait()

    def ag_copy(slot, k):
        return pltpu.make_async_remote_copy(
            src_ref=msg.at[slot], dst_ref=gath.at[slot, me],
            send_sem=ag_send.at[slot, k], recv_sem=ag_recv.at[slot, k],
            device_id=(clip, partner(k)), device_id_type=MESH,
        )

    def gather_start(slot):
        gath[slot, me] = msg[slot]
        for k in range(1, ND):
            ag_copy(slot, k).start()

    def gather_end(slot):
        def one(k, carry):
            ag_copy(slot, k).wait()
            return carry

        lax.fori_loop(1, ND, one, 0)
        every = gath[slot]
        lane = lax.broadcasted_iota(jnp.int32, (8, W), 1)
        total = jnp.sum(every, axis=0)
        mean = total * (1.0 / ND)
        away = every - mean[None]
        spread = jnp.sum(away * away, axis=0) * n_local
        square = total + pltpu.roll(spread, GROUPS, 1)
        return jnp.where(lane < GROUPS, mean, jnp.where(lane < 2 * GROUPS, square, 0.0))

    def channel_stats(j, xs):
        total = (xs[0] + xs[1]) + (xs[2] + xs[3])
        middle = total * (1.0 / R)
        away = None
        for x in xs:
            d = x - middle
            away = d * d if away is None else away + d * d
        mean = to_row(total) * (1.0 / (R * W))
        d = middle - to_cols(mean)
        means[pl.ds(j, 1), :] = mean
        sqs[pl.ds(j, 1), :] = to_row(away + d * d * float(R))

    def channel_sums(j, xs):
        total = (xs[0] + xs[1]) + (xs[2] + xs[3])
        square = (xs[0] * xs[0] + xs[1] * xs[1]) + (xs[2] * xs[2] + xs[3] * xs[3])
        mean = to_row(total) * (1.0 / (R * W))
        means[pl.ds(j, 1), :] = mean
        sqs[pl.ds(j, 1), :] = to_row(square) - mean * mean * float(R * W)

    def stats(slot):
        mean = means[...]
        d = mean - exact(mean, same[...]) * (1.0 / PER)
        inner = sqs[...] + d * d * float(R * W)
        msg[slot] = exact(mean, lanes_a[...]) * (1.0 / PER) + exact(inner, lanes_b[...])

    def coefs(slot, gain, shift):
        both = gather_end(slot)
        valid = lax.broadcasted_iota(jnp.int32, (8, W), 1) < GROUPS
        var = jnp.maximum(pltpu.roll(both, W - GROUPS, 1), 0.0) * (1.0 / (ND * n_local))
        inv = jnp.where(valid, lax.rsqrt(var + 1e-5), 0.0)
        both = exact(jnp.concatenate([inv, jnp.where(valid, both, 0.0)], axis=0), rows_g[...])
        scale = both[0:8] * gain[...].reshape(1, C)
        coef[slot, 0] = scale * 0.5
        coef[slot, 1] = (shift[...].reshape(1, C) - both[8:16] * scale) * 0.5

    def activate(buf, act, slot, f):
        sc = to_cols(coef[slot, 0, pl.ds(f, 1), :])
        sh = to_cols(coef[slot, 1, pl.ds(f, 1), :])
        for row in range(R + 2):
            h = buf[row, f].astype(F32) * sc + sh
            a = h * jnp.tanh(h) + h
            if row == 0:
                a = jnp.where(me > 0, a, 0.0)
            if row == R + 1:
                a = jnp.where(me < ND - 1, a, 0.0)
            act[:, row * W : (row + 1) * W] = a.astype(BF16)

    acts = (act0, act1)

    def split(i, carry):
        for p, buf in enumerate((wide, wide2)):
            f = i * 2 + p
            pltpu.make_async_copy(lat_in.at[f], lraw.at[f], in_sem.at[f]).wait()
        for p, buf in enumerate((wide, wide2)):
            f = i * 2 + p
            buf[...] = lraw[f].astype(F32)
            xs = [buf[pl.ds(r, C, stride=R), :] for r in range(R)]
            for r in range(R):
                x6[r + 1, f] = xs[r].astype(BF16)
            channel_stats(f, xs)
        return carry

    means[...] = jnp.zeros((8, C), F32)
    sqs[...] = jnp.zeros((8, C), F32)
    lax.fori_loop(0, 1, split, 0)
    pl.semaphore_wait(barrier, ND - 1)
    halo_start(0, 0)
    lax.fori_loop(1, FR // 2, split, 0)
    for copy in others:
        copy.start()
    same[...] = where_one(group_of((C, C), 0) == group_of((C, C), 1))
    lane = lax.broadcasted_iota(jnp.int32, (C, W), 1)
    lanes_a[...] = where_one(group_of((C, W), 0) == lane)
    lanes_b[...] = where_one(group_of((C, W), 0) + GROUPS == lane)
    stats(0)
    gather_start(0)
    for n in range(1, len(EDGES[0])):
        halo_start(0, n)

    rows_g[...] = where_one(group_of((W, C), 1) == lax.broadcasted_iota(jnp.int32, (W, C), 0))
    for copy in others:
        copy.wait()
    embed = temb[...].astype(F32)
    tact = (embed / (1.0 + jnp.exp(-embed))).astype(BF16)
    place_weights(raw1, pk1, dot_nt(tact, tw[...]) + bias1[...].reshape(1, C))
    place_weights(raw2, pk2, jnp.broadcast_to(bias2[...].reshape(1, C), (8, C)))
    orders[...] = jnp.transpose(jnp.broadcast_to(order[...].astype(F32), (2 * W, 256))).astype(jnp.int32)
    chosen[...] = jnp.zeros((256, C), F32)

    coefs(0, gain1, shift1)
    halo_wait(0, 0)
    halo_wait(0, 1)
    activate(x6, act0, 0, 0)
    for f in range(FR):
        if f in (2, 4, 6):
            if f > 2:
                stats(SLOT_TWO[f - 1])
                gather_start(SLOT_TWO[f - 1])
            halo_wait(0, f // 2 + 1)
            halo_start(1, f // 2 - 1)
        if f + 1 < FR:
            activate(x6, acts[(f + 1) % 2], 0, f + 1)
        xs = []
        for half in range(2):
            for y in conv_half(acts[f % 2], pk1, f, half):
                h = y.astype(BF16)
                h6[len(xs) + 1, f] = h
                xs.append(h.astype(F32))
        channel_sums(f, xs)
    stats(SLOT_TWO[FR - 1])

    quarter = lax.div(lax.broadcasted_iota(jnp.int32, (256, 2 * W), 1), 4)
    coefs(1, gain2, shift2)
    halo_wait(1, 0)
    gather_start(SLOT_TWO[FR - 1])
    halo_start(1, FR // 2 - 1)
    activate(h6, act0, 1, 0)
    for f in range(FR):
        if f + 1 < FR:
            slot = SLOT_TWO[f + 1]
            if SLOT_TWO[f] != slot:
                coefs(slot, gain2, shift2)
            if f % 2 == 1:
                halo_wait(1, (f + 1) // 2)
            activate(h6, acts[(f + 1) % 2], slot, f + 1)
        total = None
        for half in range(2):
            for i, y in enumerate(conv_half(acts[f % 2], pk2, f, half)):
                r = half * 2 + i
                v = y + x6[r + 1, f].astype(F32)
                resbuf[f, r] = v.astype(BF16)
                total = v if total is None else total + v
        high = total.astype(BF16)
        cols = slice(f % 2 * W, f % 2 * W + W)
        sums[0, :, cols] = high
        sums[1, :, cols] = (total - high.astype(F32)).astype(BF16)
        if f % 2 == 1:
            pick = jnp.where(orders[...] == quarter + f // 2 * (W // 2), 1.0 / 16.0, 0.0).astype(BF16)
            chosen[...] += dot_nt(pick, sums[0]) + dot_nt(pick, sums[1])

    placed = chosen[...].reshape(ND, 8, C)
    lower = jnp.concatenate([placed[:, :, 256:C], jnp.zeros((ND, 8, 512 - C), F32)], axis=2)
    tsend[...] = jnp.concatenate([placed[:, :, 0:256], lower], axis=1).astype(BF16)

    def tok_copy(k):
        return pltpu.make_async_remote_copy(
            src_ref=tsend.at[partner(k)], dst_ref=trecv.at[me],
            send_sem=tok_send.at[k], recv_sem=tok_recv.at[k],
            device_id=(clip, partner(k)), device_id_type=MESH,
        )

    def tok_wait(k, carry):
        tok_copy(k).wait()
        return carry

    for k in range(1, ND):
        tok_copy(k).start()
    trecv[me] = tsend[me]

    for f in range(FR):
        buf = (wide, wide2)[f % 2]
        for r in range(R):
            buf[pl.ds(r, C, stride=R), :] = resbuf[f, r].astype(F32)
        res[f] = buf[...].astype(BF16)

    lax.fori_loop(1, ND, tok_wait, 0)
    tok[...] = trecv[...]


def finish_kernel(res, tok, out, student, sbuf, sem):
    put = [pltpu.make_async_copy(res.at[f], out.at[f], sem.at[f]) for f in range(FR)]
    for copy in put:
        copy.start()
    t = tok[...].astype(F32)
    top = jnp.transpose(t[:, 0:8, :].reshape(256, 256))
    low = jnp.transpose(t[:, 8:16, 0:128].reshape(256, 128))
    sbuf[...] = jnp.concatenate([top, low[0 : C - 256]], axis=0).astype(BF16)
    put.append(pltpu.make_async_copy(sbuf, student.at[0], sem.at[FR]))
    put[FR].start()
    for copy in put:
        copy.wait()


def body(lat, temb, tw, gain1, shift1, w1, bias1, gain2, shift2, w2, bias2, order):
    anyspace = pl.BlockSpec(memory_space=pl.ANY)
    vm = pl.BlockSpec(memory_space=pltpu.VMEM)
    dma = pltpu.SemaphoreType.DMA
    vec = pltpu.VMEM((C,), F32)
    raw = pltpu.VMEM((9, C, C), BF16)
    edges = dma((2, len(EDGES[0]), 2))
    res, tok = pl.pallas_call(
        main_kernel,
        out_shape=(
            pltpu.VMEM((FR, C * R, W), BF16),
            pltpu.VMEM((ND, 16, 256), BF16),
        ),
        in_specs=[pl.BlockSpec(memory_space=pltpu.HBM)] * 12,
        out_specs=(vm, vm),
        scratch_shapes=[
            pltpu.VMEM((FR, C * R, W), BF16),
            pltpu.VMEM((FR, TEMB), BF16),
            pltpu.VMEM((C, TEMB), BF16),
            vec, vec, raw, vec, vec, vec, raw, vec,
            pltpu.VMEM((1, 256), jnp.int32),
            pltpu.VMEM((C * R, W), F32),
            pltpu.VMEM((C * R, W), F32),
            pltpu.VMEM((R + 2, FR, C, W), BF16),
            pltpu.VMEM((R + 2, FR, C, W), BF16),
            pltpu.VMEM((C, (R + 2) * W), BF16),
            pltpu.VMEM((C, (R + 2) * W), BF16),
            pltpu.VMEM((3 * C, DEPTH), BF16),
            pltpu.VMEM((3 * C, DEPTH), BF16),
            pltpu.VMEM((FR, R, C, W), BF16),
            pltpu.VMEM((2, C, 2 * W), BF16),
            pltpu.VMEM((8, C), F32),
            pltpu.VMEM((8, C), F32),
            pltpu.VMEM((SLOTS, ND, 8, W), F32),
            pltpu.VMEM((SLOTS, 8, W), F32),
            pltpu.VMEM((SLOTS, 2, 8, C), F32),
            pltpu.VMEM((C, C), BF16),
            pltpu.VMEM((C, W), BF16),
            pltpu.VMEM((C, W), BF16),
            pltpu.VMEM((W, C), BF16),
            pltpu.VMEM((256, 2 * W), jnp.int32),
            pltpu.VMEM((256, C), F32),
            pltpu.VMEM((ND, 16, 256), BF16),
            pltpu.VMEM((ND, 16, 256), BF16),
            dma((FR,)), dma((11,)), edges, edges,
            dma((SLOTS, ND)), dma((SLOTS, ND)), dma((ND,)), dma((ND,)),
        ],
        compiler_params=pltpu.CompilerParams(
            collective_id=0, has_side_effects=True, vmem_limit_bytes=56 * 2**20
        ),
        name="block",
    )(
        *(
            pltpu.with_memory_space_constraint(a, pltpu.HBM)
            for a in (
                lat.reshape(FR, C * R, W), temb, tw.T, gain1, shift1, w1.reshape(9, C, C), bias1,
                gain2, shift2, w2.reshape(9, C, C), bias2, order,
            )
        )
    )
    out, student = pl.pallas_call(
        finish_kernel,
        out_shape=(
            jax.ShapeDtypeStruct((FR, C * R, W), BF16),
            jax.ShapeDtypeStruct((1, C, 256), BF16),
        ),
        in_specs=[vm, vm],
        out_specs=(anyspace, anyspace),
        scratch_shapes=[pltpu.VMEM((C, 256), BF16), dma((FR + 1,))],
        compiler_params=pltpu.CompilerParams(vmem_limit_bytes=16 * 2**20),
        name="finish",
    )(
        pltpu.with_memory_space_constraint(res, pltpu.VMEM),
        pltpu.with_memory_space_constraint(tok, pltpu.VMEM),
    )
    return out.reshape(FR, C, R, W), student


def solution(mesh):
    return jax.shard_map(
        body,
        mesh=mesh,
        in_specs=(
            P("clip", None, "rows", None),
            P("clip", None),
            P(), P(), P(), P(), P(), P(), P(), P(), P(),
            P("clip", "rows"),
        ),
        out_specs=(P("clip", None, "rows", None), P("clip", None, "rows")),
        check_vma=False,
    )
```

```python
import functools

import jax
import jax.numpy as jnp
from jax import lax
from jax.experimental import pallas as pl
from jax.experimental.pallas import tpu as pltpu
from jax.sharding import PartitionSpec as P

F32 = jnp.float32
BF16 = jnp.bfloat16
C = 320
GROUPS = 32
PER = C // GROUPS
W = 128
TEMB = 1280
R = 4
FR = 8
ND = 32
EDGES = (((0, 2), (2, 1), (3, 2), (5, 2), (7, 1)), ((0, 2), (2, 2), (4, 2), (6, 2)))
SLOT_TWO = (1, 1, 1, 1, 2, 2, 2, 2)
SLOTS = 3
DEPTH = 3 * C + 32
MESH = pl.DeviceIdType.MESH


def dot(a, b):
    return jnp.dot(a, b, preferred_element_type=F32)


def dot_nt(a, b):
    return lax.dot_general(a, b, (((1,), (1,)), ((), ())), preferred_element_type=F32)


def to_row(x):
    return jnp.sum(jnp.transpose(x), axis=0, keepdims=True)


def to_cols(row):
    return jnp.transpose(jnp.broadcast_to(row, (W, C)))


def split3(a):
    high = a.astype(BF16)
    rest = a - high.astype(F32)
    mid = rest.astype(BF16)
    return jnp.concatenate([high, mid, (rest - mid.astype(F32)).astype(BF16)], axis=0)


def exact(a, ones):
    m = a.shape[0]
    y = dot(split3(a), ones)
    return y[0:m] + y[m : 2 * m] + y[2 * m : 3 * m]


def group_of(shape, dim):
    i = lax.broadcasted_iota(jnp.int32, shape, dim)
    return lax.div(i, PER)


def where_one(flags):
    return jnp.where(flags, 1.0, 0.0).astype(BF16)


def place_weights(raw, packed, offsets):
    parts = split3(offsets).astype(F32)
    parts = jnp.transpose(jnp.concatenate([parts, jnp.zeros((W - 24, C), F32)], axis=0))
    parts = parts[:, 0:32].astype(BF16)
    for b in range(3):
        rows = slice(b * C, (b + 1) * C)
        for a in range(3):
            packed[rows, a * 256 : (a + 1) * 256] = raw[a * 3 + b, :, 0:256]
        rest = [raw[a * 3 + b, :, 256:C] for a in range(3)]
        rest.append(parts if b == 1 else jnp.zeros((C, 32), BF16))
        packed[rows, 768:DEPTH] = jnp.concatenate(rest, axis=1)


def conv_half(act, packed, f, half):
    lane = lax.broadcasted_iota(jnp.int32, (C, W), 1)
    row = lax.broadcasted_iota(jnp.int32, (32, 2 * W), 0)
    mine = where_one((lax.rem(row, 8) == f) & (row < 24))
    at = [slice((half * 2 + a) * W, (half * 2 + a) * W + 2 * W) for a in range(3)]
    rhs = jnp.concatenate(
        [act[0:256, at[a]] for a in range(3)] + [act[256:C, at[a]] for a in range(3)] + [mine], axis=0
    )
    y = [dot(packed[b * C : (b + 1) * C, :], rhs) for b in range(3)]
    rows = []
    for r in range(2):
        s = slice(r * W, (r + 1) * W)
        left = jnp.where(lane == 0, 0.0, pltpu.roll(y[0][:, s], 1, 1))
        right = jnp.where(lane == W - 1, 0.0, pltpu.roll(y[2][:, s], W - 1, 1))
        rows.append(y[1][:, s] + left + right)
    return rows


def main_kernel(
    lat_in, temb_in, tw_in, gain1_in, shift1_in, w1_in, bias1_in, gain2_in, shift2_in, w2_in, bias2_in, order_in,
    res, tok,
    lraw, temb, tw, gain1, shift1, raw1, bias1, gain2, shift2, raw2, bias2, order,
    wide, wide2, x6, h6, act0, act1, pk1, pk2, resbuf, sums,
    means, sqs, gath, msg, coef, same, lanes_a, lanes_b, rows_g, orders, chosen, tsend, trecv,
    in_sem, small_sem, halo_send, halo_recv, ag_send, ag_recv, tok_send, tok_recv,
):
    clip, me = lax.axis_index("clip"), lax.axis_index("rows")
    up, down = lax.rem(me + ND - 1, ND), lax.rem(me + 1, ND)
    n_local = float(PER * R * W)

    def partner(k):
        return lax.rem(me + k, ND)

    fetch = [pltpu.make_async_copy(lat_in.at[f], lraw.at[f], in_sem.at[f]) for f in range(FR)]
    for copy in fetch:
        copy.start()

    barrier = pltpu.get_barrier_semaphore()

    def greet(k, carry):
        pl.semaphore_signal(barrier, inc=1, device_id=(clip, partner(k)), device_id_type=MESH)
        return carry

    lax.fori_loop(1, ND, greet, 0)

    others = [
        (temb_in, temb), (tw_in, tw), (bias1_in, bias1), (w1_in, raw1), (gain1_in, gain1), (shift1_in, shift1),
        (bias2_in, bias2), (w2_in, raw2), (gain2_in, gain2), (shift2_in, shift2), (order_in, order),
    ]
    others = [pltpu.make_async_copy(a, b, small_sem.at[i]) for i, (a, b) in enumerate(others)]
    for copy in others:
        copy.start()

    def halo_copies(stage, n):
        buf = (x6, h6)[stage]
        frames = pl.ds(*EDGES[stage][n])
        return [
            pltpu.make_async_remote_copy(
                src_ref=buf.at[src, frames], dst_ref=buf.at[dst, frames],
                send_sem=halo_send.at[stage, n, i], recv_sem=halo_recv.at[stage, n, i],
                device_id=(clip, to), device_id_type=MESH,
            )
            for i, (src, dst, to) in enumerate(((1, 5, up), (4, 0, down)))
        ]

    def halo_start(stage, n):
        for copy in halo_copies(stage, n):
            copy.start()

    def halo_wait(stage, n):
        for copy in halo_copies(stage, n):
            copy.wait()

    def ag_copy(slot, k):
        return pltpu.make_async_remote_copy(
            src_ref=msg.at[slot], dst_ref=gath.at[slot, me],
            send_sem=ag_send.at[slot, k], recv_sem=ag_recv.at[slot, k],
            device_id=(clip, partner(k)), device_id_type=MESH,
        )

    def gather_start(slot):
        gath[slot, me] = msg[slot]
        for k in range(1, ND):
            ag_copy(slot, k).start()

    def gather_end(slot):
        def one(k, carry):
            ag_copy(slot, k).wait()
            return carry

        lax.fori_loop(1, ND, one, 0)
        every = gath[slot]
        lane = lax.broadcasted_iota(jnp.int32, (8, W), 1)
        total = jnp.sum(every, axis=0)
        mean = total * (1.0 / ND)
        away = every - mean[None]
        spread = jnp.sum(away * away, axis=0) * n_local
        square = total + pltpu.roll(spread, GROUPS, 1)
        return jnp.where(lane < GROUPS, mean, jnp.where(lane < 2 * GROUPS, square, 0.0))

    def channel_stats(j, xs):
        total = (xs[0] + xs[1]) + (xs[2] + xs[3])
        middle = total * (1.0 / R)
        away = None
        for x in xs:
            d = x - middle
            away = d * d if away is None else away + d * d
        mean = to_row(total) * (1.0 / (R * W))
        d = middle - to_cols(mean)
        means[pl.ds(j, 1), :] = mean
        sqs[pl.ds(j, 1), :] = to_row(away + d * d * float(R))

    def channel_sums(j, xs):
        total = (xs[0] + xs[1]) + (xs[2] + xs[3])
        square = (xs[0] * xs[0] + xs[1] * xs[1]) + (xs[2] * xs[2] + xs[3] * xs[3])
        mean = to_row(total) * (1.0 / (R * W))
        means[pl.ds(j, 1), :] = mean
        sqs[pl.ds(j, 1), :] = to_row(square) - mean * mean * float(R * W)

    def stats(slot):
        mean = means[...]
        d = mean - exact(mean, same[...]) * (1.0 / PER)
        inner = sqs[...] + d * d * float(R * W)
        msg[slot] = exact(mean, lanes_a[...]) * (1.0 / PER) + exact(inner, lanes_b[...])

    def coefs(slot, gain, shift):
        both = gather_end(slot)
        valid = lax.broadcasted_iota(jnp.int32, (8, W), 1) < GROUPS
        var = jnp.maximum(pltpu.roll(both, W - GROUPS, 1), 0.0) * (1.0 / (ND * n_local))
        inv = jnp.where(valid, lax.rsqrt(var + 1e-5), 0.0)
        both = exact(jnp.concatenate([inv, jnp.where(valid, both, 0.0)], axis=0), rows_g[...])
        scale = both[0:8] * gain[...].reshape(1, C)
        coef[slot, 0] = scale * 0.5
        coef[slot, 1] = (shift[...].reshape(1, C) - both[8:16] * scale) * 0.5

    def activate(buf, act, slot, f):
        sc = to_cols(coef[slot, 0, pl.ds(f, 1), :])
        sh = to_cols(coef[slot, 1, pl.ds(f, 1), :])
        for row in range(R + 2):
            h = buf[row, f].astype(F32) * sc + sh
            a = h * jnp.tanh(h) + h
            if row == 0:
                a = jnp.where(me > 0, a, 0.0)
            if row == R + 1:
                a = jnp.where(me < ND - 1, a, 0.0)
            act[:, row * W : (row + 1) * W] = a.astype(BF16)

    acts = (act0, act1)

    def split(i, carry):
        for p, buf in enumerate((wide, wide2)):
            f = i * 2 + p
            pltpu.make_async_copy(lat_in.at[f], lraw.at[f], in_sem.at[f]).wait()
        for p, buf in enumerate((wide, wide2)):
            f = i * 2 + p
            buf[...] = lraw[f].astype(F32)
            xs = [buf[pl.ds(r, C, stride=R), :] for r in range(R)]
            for r in range(R):
                x6[r + 1, f] = xs[r].astype(BF16)
            channel_stats(f, xs)
        return carry

    same[...] = where_one(group_of((C, C), 0) == group_of((C, C), 1))
    lane = lax.broadcasted_iota(jnp.int32, (C, W), 1)
    lanes_a[...] = where_one(group_of((C, W), 0) == lane)
    lanes_b[...] = where_one(group_of((C, W), 0) + GROUPS == lane)
    means[...] = jnp.zeros((8, C), F32)
    sqs[...] = jnp.zeros((8, C), F32)
    lax.fori_loop(0, 1, split, 0)
    pl.semaphore_wait(barrier, ND - 1)
    halo_start(0, 0)
    lax.fori_loop(1, FR // 2, split, 0)
    stats(0)
    gather_start(0)
    for n in range(1, len(EDGES[0])):
        halo_start(0, n)

    rows_g[...] = where_one(group_of((W, C), 1) == lax.broadcasted_iota(jnp.int32, (W, C), 0))
    for copy in others:
        copy.wait()
    embed = temb[...].astype(F32)
    tact = (embed / (1.0 + jnp.exp(-embed))).astype(BF16)
    place_weights(raw1, pk1, dot_nt(tact, tw[...]) + bias1[...].reshape(1, C))
    place_weights(raw2, pk2, jnp.broadcast_to(bias2[...].reshape(1, C), (8, C)))
    orders[...] = jnp.transpose(jnp.broadcast_to(order[...].astype(F32), (2 * W, 256))).astype(jnp.int32)
    chosen[...] = jnp.zeros((256, C), F32)

    coefs(0, gain1, shift1)
    halo_wait(0, 0)
    halo_wait(0, 1)
    activate(x6, act0, 0, 0)
    for f in range(FR):
        if f in (2, 4, 6):
            if SLOT_TWO[f - 1] != SLOT_TWO[f]:
                stats(SLOT_TWO[f - 1])
                gather_start(SLOT_TWO[f - 1])
            halo_wait(0, f // 2 + 1)
            halo_start(1, f // 2 - 1)
        if f + 1 < FR:
            activate(x6, acts[(f + 1) % 2], 0, f + 1)
        xs = []
        for half in range(2):
            for y in conv_half(acts[f % 2], pk1, f, half):
                h = y.astype(BF16)
                h6[len(xs) + 1, f] = h
                xs.append(h.astype(F32))
        channel_sums(f, xs)
    stats(SLOT_TWO[FR - 1])

    quarter = lax.div(lax.broadcasted_iota(jnp.int32, (256, 2 * W), 1), 4)
    coefs(1, gain2, shift2)
    halo_wait(1, 0)
    gather_start(SLOT_TWO[FR - 1])
    halo_start(1, FR // 2 - 1)
    activate(h6, act0, 1, 0)
    for f in range(FR):
        if f + 1 < FR:
            slot = SLOT_TWO[f + 1]
            if SLOT_TWO[f] != slot:
                coefs(slot, gain2, shift2)
            if f % 2 == 1:
                halo_wait(1, (f + 1) // 2)
            activate(h6, acts[(f + 1) % 2], slot, f + 1)
        total = None
        for half in range(2):
            for i, y in enumerate(conv_half(acts[f % 2], pk2, f, half)):
                r = half * 2 + i
                v = y + x6[r + 1, f].astype(F32)
                resbuf[f, r] = v.astype(BF16)
                total = v if total is None else total + v
        high = total.astype(BF16)
        cols = slice(f % 2 * W, f % 2 * W + W)
        sums[0, :, cols] = high
        sums[1, :, cols] = (total - high.astype(F32)).astype(BF16)
        if f % 2 == 1:
            pick = jnp.where(orders[...] == quarter + f // 2 * (W // 2), 1.0 / 16.0, 0.0).astype(BF16)
            chosen[...] += dot_nt(pick, sums[0]) + dot_nt(pick, sums[1])

    placed = chosen[...].reshape(ND, 8, C)
    lower = jnp.concatenate([placed[:, :, 256:C], jnp.zeros((ND, 8, 512 - C), F32)], axis=2)
    tsend[...] = jnp.concatenate([placed[:, :, 0:256], lower], axis=1).astype(BF16)

    def tok_copy(k):
        return pltpu.make_async_remote_copy(
            src_ref=tsend.at[partner(k)], dst_ref=trecv.at[me],
            send_sem=tok_send.at[k], recv_sem=tok_recv.at[k],
            device_id=(clip, partner(k)), device_id_type=MESH,
        )

    def tok_wait(k, carry):
        tok_copy(k).wait()
        return carry

    trecv[me] = tsend[me]
    for k in range(1, ND):
        tok_copy(k).start()

    def weave(i, carry):
        for p, buf in enumerate((wide, wide2)):
            for r in range(R):
                buf[pl.ds(r, C, stride=R), :] = resbuf[i * 2 + p, r].astype(F32)
            res[i * 2 + p] = buf[...].astype(BF16)
        return carry

    lax.fori_loop(0, FR // 2, weave, 0)

    lax.fori_loop(1, ND, tok_wait, 0)
    tok[...] = trecv[...]


def finish_kernel(res, tok, out, student, sbuf, sem):
    put = [pltpu.make_async_copy(res.at[f], out.at[f], sem.at[f]) for f in range(FR)]
    for copy in put:
        copy.start()
    t = tok[...].astype(F32)
    top = jnp.transpose(t[:, 0:8, :].reshape(256, 256))
    low = jnp.transpose(t[:, 8:16, 0:128].reshape(256, 128))
    sbuf[...] = jnp.concatenate([top, low[0 : C - 256]], axis=0).astype(BF16)
    put.append(pltpu.make_async_copy(sbuf, student.at[0], sem.at[FR]))
    put[FR].start()
    for copy in put:
        copy.wait()


def body(lat, temb, tw, gain1, shift1, w1, bias1, gain2, shift2, w2, bias2, order):
    anyspace = pl.BlockSpec(memory_space=pl.ANY)
    vm = pl.BlockSpec(memory_space=pltpu.VMEM)
    dma = pltpu.SemaphoreType.DMA
    vec = pltpu.VMEM((C,), F32)
    raw = pltpu.VMEM((9, C, C), BF16)
    edges = dma((2, len(EDGES[0]), 2))
    res, tok = pl.pallas_call(
        main_kernel,
        out_shape=(
            pltpu.VMEM((FR, C * R, W), BF16),
            pltpu.VMEM((ND, 16, 256), BF16),
        ),
        in_specs=[pl.BlockSpec(memory_space=pltpu.HBM)] * 12,
        out_specs=(vm, vm),
        scratch_shapes=[
            pltpu.VMEM((FR, C * R, W), BF16),
            pltpu.VMEM((FR, TEMB), BF16),
            pltpu.VMEM((C, TEMB), BF16),
            vec, vec, raw, vec, vec, vec, raw, vec,
            pltpu.VMEM((1, 256), jnp.int32),
            pltpu.VMEM((C * R, W), F32),
            pltpu.VMEM((C * R, W), F32),
            pltpu.VMEM((R + 2, FR, C, W), BF16),
            pltpu.VMEM((R + 2, FR, C, W), BF16),
            pltpu.VMEM((C, (R + 2) * W), BF16),
            pltpu.VMEM((C, (R + 2) * W), BF16),
            pltpu.VMEM((3 * C, DEPTH), BF16),
            pltpu.VMEM((3 * C, DEPTH), BF16),
            pltpu.VMEM((FR, R, C, W), BF16),
            pltpu.VMEM((2, C, 2 * W), BF16),
            pltpu.VMEM((8, C), F32),
            pltpu.VMEM((8, C), F32),
            pltpu.VMEM((SLOTS, ND, 8, W), F32),
            pltpu.VMEM((SLOTS, 8, W), F32),
            pltpu.VMEM((SLOTS, 2, 8, C), F32),
            pltpu.VMEM((C, C), BF16),
            pltpu.VMEM((C, W), BF16),
            pltpu.VMEM((C, W), BF16),
            pltpu.VMEM((W, C), BF16),
            pltpu.VMEM((256, 2 * W), jnp.int32),
            pltpu.VMEM((256, C), F32),
            pltpu.VMEM((ND, 16, 256), BF16),
            pltpu.VMEM((ND, 16, 256), BF16),
            dma((FR,)), dma((11,)), edges, edges,
            dma((SLOTS, ND)), dma((SLOTS, ND)), dma((ND,)), dma((ND,)),
        ],
        compiler_params=pltpu.CompilerParams(
            collective_id=0, has_side_effects=True, vmem_limit_bytes=56 * 2**20
        ),
        name="block",
    )(
        *(
            pltpu.with_memory_space_constraint(a, pltpu.HBM)
            for a in (
                lat.reshape(FR, C * R, W), temb, tw.T, gain1, shift1, w1.reshape(9, C, C), bias1,
                gain2, shift2, w2.reshape(9, C, C), bias2, order,
            )
        )
    )
    out, student = pl.pallas_call(
        finish_kernel,
        out_shape=(
            jax.ShapeDtypeStruct((FR, C * R, W), BF16),
            jax.ShapeDtypeStruct((1, C, 256), BF16),
        ),
        in_specs=[vm, vm],
        out_specs=(anyspace, anyspace),
        scratch_shapes=[pltpu.VMEM((C, 256), BF16), dma((FR + 1,))],
        compiler_params=pltpu.CompilerParams(vmem_limit_bytes=16 * 2**20),
        name="finish",
    )(
        pltpu.with_memory_space_constraint(res, pltpu.VMEM),
        pltpu.with_memory_space_constraint(tok, pltpu.VMEM),
    )
    return out.reshape(FR, C, R, W), student


def solution(mesh):
    return jax.shard_map(
        body,
        mesh=mesh,
        in_specs=(
            P("clip", None, "rows", None),
            P("clip", None),
            P(), P(), P(), P(), P(), P(), P(), P(), P(),
            P("clip", "rows"),
        ),
        out_specs=(P("clip", None, "rows", None), P("clip", None, "rows")),
        check_vma=False,
    )
```
